32 devices in a mesh: tm: 4 (over y, x), rows: 8 (over z, core).
Axes of the slice: x: 2, y: 2, z: 4, core: 2. Of those that a mesh axis runs over, the one named last changes fastest.
Arguments:
- latents: bfloat16 [64, 16, 10240], P('tm', 'rows')
- video_patch_choice: int32 [2], replicated, may hold values from 0 to 31
- video_patch_degrees: int32 [2], replicated, may hold values from 16 to 64, as said below
- first_norm_gain: float32 [320], replicated, may hold values from 0.5 to 1.5
- first_norm_shift: float32 [320], replicated, may hold values from -3 to 3
- first_conv_weight: bfloat16 [3, 3, 320, 320], replicated, may hold values from -0.109375 to 0.109375
- timestep_bias: float32 [320], replicated, may hold values from -3 to 3
- second_norm_gain: float32 [320], replicated, may hold values from 0.5 to 1.5
- second_norm_shift: float32 [320], replicated, may hold values from -3 to 3
- second_conv_weight: bfloat16 [3, 3, 320, 320], replicated, may hold values from -0.109375 to 0.109375
- second_conv_bias: float32 [320], replicated, may hold values from -3 to 3
- third_norm_gain: float32 [320], replicated, may hold values from 0.5 to 1.5
- third_norm_shift: float32 [320], replicated, may hold values from -3 to 3
- input_projection_weight: bfloat16 [320, 320], replicated, may hold values from -0.3125 to 0.3125
- input_projection_bias: float32 [320], replicated, may hold values from -3 to 3
- layer_norm_gain: float32 [320], replicated, may hold values from 0.5 to 1.5
- layer_norm_shift: float32 [320], replicated, may hold values from -3 to 3
- attention_weight: bfloat16 [4, 320, 320], replicated, may hold values from -0.3125 to 0.3125
- attention_output_bias: float32 [320], replicated, may hold values from -3 to 3
- patch_lowering_store: bfloat16 [32, 4, 320, 64], P(('tm', 'rows')), may hold values from -0.3125 to 0.3125
- patch_raising_store: bfloat16 [32, 4, 64, 320], P(('tm', 'rows')), may hold values from -0.75 to 0.75
- output_projection_weight: bfloat16 [320, 320], replicated, may hold values from -0.3125 to 0.3125
- output_projection_bias: float32 [320], replicated, may hold values from -3 to 3
Outputs:
- block_out: bfloat16 [64, 16, 10240], P('tm', 'rows')
The draws below stay inside these ranges and needn't reach their ends.
Inputs may be any that keep to these rules, and one draw needn't show every extreme that they name: video_patch_degrees of at least one clip equals 64.
All inputs are finite; a program needn't handle non-finite values.
Results may differ from the reference program's by a relative error of at most 0.019.
Values may be sent and summed in bfloat16 or wider, within the bound.
A program may use at most 128 MiB of HBM per device.

```python
import math
import jax
import jax.numpy as jnp
from jax import lax

FEATURE_WIDTH = 320
GROUPS = 32
HEADS = 8
PATCH_DEGREE_TOP = 64
W = 32
CLIP_LEN = 32
FRAMES = 64
HEIGHT = 16
VIDEO_JOBS = 2
HD = 40
MOTION_PATCHES = 32


def draw_latents(key, part):
    key = jax.random.fold_in(key, 11)
    leading_entry, second = jax.random.split(key, 2)
    ramp = 0.5 + jnp.arange(HEIGHT, dtype=jnp.float32) / max(HEIGHT - 1, 1)
    rough = jax.random.uniform(second, (FRAMES, HEIGHT, 1), jnp.float32, 0.6, 1.4)
    base_result = jax.random.normal(leading_entry, (FRAMES, HEIGHT, W * FEATURE_WIDTH), jnp.float32)
    return (base_result * ramp[None, :, None] * rough).astype(jnp.bfloat16)


def draw_video_patch_degrees(key, part):
    key = jax.random.fold_in(key, 12)
    leading_entry, second = jax.random.split(key, 2)
    degree_list = jax.random.randint(leading_entry, (VIDEO_JOBS,), PATCH_DEGREE_TOP // 4, PATCH_DEGREE_TOP + 1)
    picked_patch = jax.random.randint(second, (), 0, VIDEO_JOBS)
    return jnp.where(jnp.arange(VIDEO_JOBS, dtype=jnp.int32) == picked_patch, PATCH_DEGREE_TOP, degree_list).astype(jnp.int32)


def levels(stream_key, dims, cuts, least, high):
    factor_of = 1.0
    for axis_at, shards_of in cuts:
        draws = jax.random.uniform(jax.random.fold_in(jax.random.fold_in(stream_key, 6), axis_at), (shards_of,), jnp.float32, least / len(cuts), high / len(cuts))
        factor_of = factor_of * jnp.repeat(jnp.exp(draws), dims[axis_at] // shards_of).reshape((-1,) + (1,) * (len(dims) - 1 - axis_at))
    return factor_of


def noise(key, extent, spread, limit, pieces=(), kind=jnp.bfloat16):
    level = levels(key, extent, pieces, -0.22, 0.18) if pieces else 1.0
    drawn = jax.random.normal(key, extent, jnp.float32) * spread * level
    return jnp.minimum(jnp.maximum(drawn, -limit), limit).astype(kind)


def setup_inputs(seed: int = 0) -> dict:
    splits = jax.random.split(jax.random.key(seed), 24)
    latents = draw_latents(jax.random.fold_in(splits[23], 71), 0)
    video_patch_choice = jax.random.randint(splits[1], (VIDEO_JOBS,), 0, MOTION_PATCHES).astype(jnp.int32)
    video_patch_degrees = draw_video_patch_degrees(jax.random.fold_in(splits[23], 71), 0)
    first_norm_gain = jnp.clip(1.0 + 0.1 * jax.random.normal(splits[3], (FEATURE_WIDTH,), jnp.float32), 0.5, 1.5)
    first_norm_shift = noise(splits[4], (FEATURE_WIDTH,), 0.5, 3.0, (), jnp.float32)
    first_conv_weight = noise(splits[5], (3, 3, FEATURE_WIDTH, FEATURE_WIDTH), (9 * FEATURE_WIDTH) ** -0.5, 0.109375)
    timestep_bias = noise(splits[6], (FEATURE_WIDTH,), 0.5, 3.0, (), jnp.float32)
    second_norm_gain = jnp.clip(1.0 + 0.1 * jax.random.normal(splits[7], (FEATURE_WIDTH,), jnp.float32), 0.5, 1.5)
    second_norm_shift = noise(splits[8], (FEATURE_WIDTH,), 0.5, 3.0, (), jnp.float32)
    second_conv_weight = noise(splits[9], (3, 3, FEATURE_WIDTH, FEATURE_WIDTH), (9 * FEATURE_WIDTH) ** -0.5, 0.109375)
    second_conv_bias = noise(splits[10], (FEATURE_WIDTH,), 0.5, 3.0, (), jnp.float32)
    third_norm_gain = jnp.clip(1.0 + 0.1 * jax.random.normal(splits[11], (FEATURE_WIDTH,), jnp.float32), 0.5, 1.5)
    third_norm_shift = noise(splits[12], (FEATURE_WIDTH,), 0.5, 3.0, (), jnp.float32)
    input_projection_weight = noise(splits[13], (FEATURE_WIDTH, FEATURE_WIDTH), FEATURE_WIDTH ** -0.5, 0.3125)
    input_projection_bias = noise(splits[14], (FEATURE_WIDTH,), 0.5, 3.0, (), jnp.float32)
    layer_norm_gain = jnp.clip(1.0 + 0.1 * jax.random.normal(splits[15], (FEATURE_WIDTH,), jnp.float32), 0.5, 1.5)
    layer_norm_shift = noise(splits[16], (FEATURE_WIDTH,), 0.5, 3.0, (), jnp.float32)
    attention_weight = noise(splits[17], (4, FEATURE_WIDTH, FEATURE_WIDTH), FEATURE_WIDTH ** -0.5, 0.3125)
    attention_output_bias = noise(splits[18], (FEATURE_WIDTH,), 0.5, 3.0, (), jnp.float32)
    patch_lowering_store = noise(splits[19], (MOTION_PATCHES, 4, FEATURE_WIDTH, PATCH_DEGREE_TOP), FEATURE_WIDTH ** -0.5, 0.3125, ((0, 32),))
    patch_raising_store = noise(splits[20], (MOTION_PATCHES, 4, PATCH_DEGREE_TOP, FEATURE_WIDTH), PATCH_DEGREE_TOP ** -0.5, 0.75, ((0, 32),))
    output_projection_weight = noise(splits[21], (FEATURE_WIDTH, FEATURE_WIDTH), FEATURE_WIDTH ** -0.5, 0.3125)
    output_projection_bias = noise(splits[22], (FEATURE_WIDTH,), 0.5, 3.0, (), jnp.float32)
    return dict(latents=latents, video_patch_choice=video_patch_choice, video_patch_degrees=video_patch_degrees, first_norm_gain=first_norm_gain, first_norm_shift=first_norm_shift, first_conv_weight=first_conv_weight, timestep_bias=timestep_bias, second_norm_gain=second_norm_gain, second_norm_shift=second_norm_shift, second_conv_weight=second_conv_weight, second_conv_bias=second_conv_bias, third_norm_gain=third_norm_gain, third_norm_shift=third_norm_shift, input_projection_weight=input_projection_weight, input_projection_bias=input_projection_bias, layer_norm_gain=layer_norm_gain, layer_norm_shift=layer_norm_shift, attention_weight=attention_weight, attention_output_bias=attention_output_bias, patch_lowering_store=patch_lowering_store, patch_raising_store=patch_raising_store, output_projection_weight=output_projection_weight, output_projection_bias=output_projection_bias)


EPS = 1e-05

def group_norm(v, gain, shift):
    rows, cols = (v.shape[0], v.shape[1])
    parts = v.reshape(rows * cols, GROUPS, FEATURE_WIDTH // GROUPS)
    count = rows * cols * (FEATURE_WIDTH // GROUPS)
    mean = lax.optimization_barrier(jnp.sum(parts, axis=(0, 2))) / count
    var = lax.optimization_barrier(jnp.sum(parts * parts, axis=(0, 2))) / count - mean * mean
    normed = (parts - mean[None, :, None]) * lax.rsqrt(var + EPS)[None, :, None]
    return normed.reshape(v.shape) * gain + shift

def positional(times):
    index = jnp.arange(FEATURE_WIDTH, dtype=jnp.int32)
    freq = jnp.exp(-(index // 2 * 2).astype(jnp.float32) * (math.log(10000.0) / FEATURE_WIDTH))
    angle = times[:, None] * freq[None, :]
    return jnp.where(index[None, :] % 2 == 0, jnp.sin(angle), jnp.cos(angle))

def conv_same(act, kernel):
    out = lax.conv_general_dilated(act[None], kernel, (1, 1), 'SAME', dimension_numbers=('NHWC', 'HWIO', 'NHWC'), preferred_element_type=jnp.float32)
    return out[0]

def reference(latents, video_patch_choice, video_patch_degrees, first_norm_gain, first_norm_shift, first_conv_weight, timestep_bias, second_norm_gain, second_norm_shift, second_conv_weight, second_conv_bias, third_norm_gain, third_norm_shift, input_projection_weight, input_projection_bias, layer_norm_gain, layer_norm_shift, attention_weight, attention_output_bias, patch_lowering_store, patch_raising_store, output_projection_weight, output_projection_bias):
    frame_times = (jnp.arange(FRAMES, dtype=jnp.int32) % CLIP_LEN).astype(jnp.float32)

    def frame_part(pair):
        frame, stamp = pair
        xin = frame.reshape(HEIGHT, W, FEATURE_WIDTH).astype(jnp.float32)
        act1 = jax.nn.silu(group_norm(xin, first_norm_gain, first_norm_shift)).astype(jnp.bfloat16)
        hid1 = (conv_same(act1, first_conv_weight) + timestep_bias).astype(jnp.bfloat16)
        act2 = jax.nn.silu(group_norm(hid1.astype(jnp.float32), second_norm_gain, second_norm_shift)).astype(jnp.bfloat16)
        res = (xin + conv_same(act2, second_conv_weight) + second_conv_bias).astype(jnp.bfloat16)
        normed = group_norm(res.astype(jnp.float32), third_norm_gain, third_norm_shift).astype(jnp.bfloat16)
        proj = (jnp.dot(normed.reshape(-1, FEATURE_WIDTH), input_projection_weight, preferred_element_type=jnp.float32) + input_projection_bias).astype(jnp.bfloat16)
        pf = proj.astype(jnp.float32)
        centre = pf - lax.optimization_barrier(jnp.mean(pf, axis=-1, keepdims=True))
        layer = centre * lax.rsqrt(lax.optimization_barrier(jnp.mean(centre * centre, axis=-1, keepdims=True)) + EPS) * layer_norm_gain + layer_norm_shift
        normal_in = (layer + positional(stamp[None])).astype(jnp.bfloat16)
        return (res, proj.reshape(HEIGHT, W, FEATURE_WIDTH), normal_in.reshape(HEIGHT, W, FEATURE_WIDTH))
    res_all, proj_all, norm_all = lax.map(frame_part, (latents, frame_times))
    degree_filter = (jnp.arange(PATCH_DEGREE_TOP, dtype=jnp.int32)[None, :] < video_patch_degrees[:, None]).astype(jnp.bfloat16)
    down_factors = patch_lowering_store[video_patch_choice] * degree_filter[:, None, None, :]
    up_factors = patch_raising_store[video_patch_choice]
    scale = 1.0 / math.sqrt(HD)

    def project(src, projection_index):
        base_result = jnp.dot(src.reshape(-1, FEATURE_WIDTH), attention_weight[projection_index], preferred_element_type=jnp.float32).reshape(src.shape)
        low = jnp.einsum('kfwc,kcr->kfwr', src.astype(jnp.float32), down_factors[:, projection_index].astype(jnp.float32)).astype(jnp.bfloat16)
        return base_result + jnp.einsum('kfwr,krc->kfwc', low.astype(jnp.float32), up_factors[:, projection_index].astype(jnp.float32))

    def row_part(triple):
        res, proj, normal_in = triple
        rank_limited = normal_in.reshape(VIDEO_JOBS, CLIP_LEN, W, FEATURE_WIDTH)
        heads_shape = (VIDEO_JOBS, CLIP_LEN, W, HEADS, HD)
        query = project(rank_limited, 0).astype(jnp.bfloat16).reshape(heads_shape)
        keys = project(rank_limited, 1).astype(jnp.bfloat16).reshape(heads_shape)
        values = project(rank_limited, 2).astype(jnp.bfloat16).reshape(heads_shape)
        scores = jnp.einsum('kfwhd,kgwhd->kwhfg', query.astype(jnp.float32), keys.astype(jnp.float32)) * scale
        weights = jax.nn.softmax(scores, axis=-1).astype(jnp.bfloat16)
        attended = jnp.einsum('kwhfg,kgwhd->kfwhd', weights.astype(jnp.float32), values.astype(jnp.float32)).astype(jnp.bfloat16)
        attended = attended.reshape(VIDEO_JOBS, CLIP_LEN, W, FEATURE_WIDTH)
        mixed = (proj.reshape(VIDEO_JOBS, CLIP_LEN, W, FEATURE_WIDTH).astype(jnp.float32) + project(attended, 3) + attention_output_bias).astype(jnp.bfloat16)
        final = res.astype(jnp.float32) + jnp.dot(mixed.reshape(-1, FEATURE_WIDTH), output_projection_weight, preferred_element_type=jnp.float32).reshape(FRAMES, W, FEATURE_WIDTH) + output_projection_bias
        return final.astype(jnp.bfloat16)
    outs = lax.map(row_part, (jnp.moveaxis(res_all, 1, 0), jnp.moveaxis(proj_all, 1, 0), jnp.moveaxis(norm_all, 1, 0)))
    return jnp.moveaxis(outs, 0, 1).reshape(FRAMES, HEIGHT, W * FEATURE_WIDTH)
```

```python
import functools
import math

import jax
import jax.numpy as jnp
import numpy as np
from jax import lax
from jax.experimental import pallas as pl
from jax.experimental.pallas import tpu as pltpu
from jax.sharding import PartitionSpec as P

C = 320
GROUPS = 32
GS = 10
HEADS = 8
RANK = 64
W = 32
CLIP_LEN = 32
HD = 40
EPS = 1e-05
F = 16
PIECE = 16
PANEL_ROWS = 8 * RANK
CHUNK = 16
SUB = 8
MESH = pl.DeviceIdType.MESH
F32 = jnp.float32
BF16 = jnp.bfloat16
EXACT = lax.Precision.HIGHEST


def positions():
    index = np.arange(C)
    freq = np.exp(-(index // 2 * 2) * (math.log(10000.0) / C))
    angle = np.arange(CLIP_LEN)[:, None] * freq[None, :]
    return np.where(index[None, :] % 2 == 0, np.sin(angle), np.cos(angle)).astype(np.float32)


def dot(a, b, dims=((1,), (0,)), precision=None):
    return lax.dot_general(a, b, (dims, ((), ())), preferred_element_type=F32, precision=precision)


def silu(v):
    return 0.5 * v * (1.0 + jnp.tanh(0.5 * v))


def kernel(
    nt, nr, strip, clips,
    choice, degrees,
    xt, vec, pe, k1, k2, wi, wa, wo, panel,
    out,
    xs, xh, hs, hh, act, res, proj, nown, npart, ssrc, sland, land1, src2, land2, weff, ot, att,
    hx_s, hx_r, hh_s, hh_r, st_s, st_r, l1_s, l1_r, l2_s, l2_r, n_s, n_r,
):
    n = nt * nr
    pieces = PANEL_ROWS // PIECE
    holders = min(pieces, n)
    my_t = lax.axis_index("tm")
    my_r = lax.axis_index("rows")
    me = my_t * nr + my_r
    side = lax.rem(my_t, 2)
    partner = my_t + 1 - 2 * side
    my_clip = my_t // 2
    count = float(strip * nr * W * GS)
    has_up = my_r > 0
    has_down = my_r < nr - 1

    barrier = pltpu.get_barrier_semaphore()

    def greet(off, carry):
        dst = lax.rem(me + off, n)
        pl.semaphore_signal(barrier, inc=1, device_id=(dst // nr, lax.rem(dst, nr)), device_id_type=MESH)
        return carry

    lax.fori_loop(1, n, greet, 0)

    row = lambda i: vec[i : i + 1, :]
    gc = lax.broadcasted_iota(jnp.int32, (C, 128), 0)
    gg = lax.broadcasted_iota(jnp.int32, (C, 128), 1) * GS
    to_first = ((gc >= gg) & (gc < gg + GS)).astype(F32)
    gg2 = gg - GROUPS * GS
    to_second = ((gc >= gg2) & (gc < gg2 + GS)).astype(F32)

    def unpack(p, carry):
        total, square = carry
        for r in range(strip):
            two = xt[r, :, pl.ds(pl.multiple_of(p * 2 * C, 128), 2 * C)]
            for i in range(2):
                one = two[:, i * C : (i + 1) * C]
                xs[r, 2 * p + i] = one
                wide = one.astype(F32)
                total = total + wide
                square = square + wide * wide
        return total, square

    zero = jnp.zeros((F, C), F32)

    def stat_copy(i, off):
        dst = lax.rem(my_r + off, nr)
        return pltpu.make_async_remote_copy(
            src_ref=ssrc.at[i], dst_ref=sland.at[i, my_r],
            send_sem=st_s.at[i, off], recv_sem=st_r.at[i, my_r],
            device_id=(my_t, dst), device_id_type=MESH)

    def stat_wait(i, off):
        src = lax.rem(my_r + off, nr)
        return pltpu.make_async_remote_copy(
            src_ref=ssrc.at[i], dst_ref=sland.at[i, src],
            send_sem=st_s.at[i, off], recv_sem=st_r.at[i, src],
            device_id=(my_t, src), device_id_type=MESH)

    def put_stats(i, total, square):
        mine = dot(total, to_first, precision=EXACT) + dot(square, to_second, precision=EXACT)
        ssrc[i] = mine
        sland[i, my_r] = mine

    def send_stats(i):
        def step(off, carry):
            stat_copy(i, off).start()
            return carry
        lax.fori_loop(1, nr, step, 0)

    def get_stats(i, gain, shift):
        def step(off, carry):
            stat_wait(i, off).wait_recv()
            return carry
        lax.fori_loop(1, nr, step, 0)
        total = sland[i, 0]
        for s in range(1, nr):
            total = total + sland[i, s]
        total = total * (1.0 / count)
        mean = dot(total, to_first, ((1,), (1,)), EXACT)
        var = dot(total, to_second, ((1,), (1,)), EXACT) - mean * mean
        scale = lax.rsqrt(var + EPS) * gain
        return scale, shift - mean * scale

    def halo(src, dst, send, recv, up):
        if up:
            return pltpu.make_async_remote_copy(
                src_ref=src.at[0], dst_ref=dst.at[1], send_sem=send.at[0], recv_sem=recv.at[1],
                device_id=(my_t, my_r - 1), device_id_type=MESH)
        return pltpu.make_async_remote_copy(
            src_ref=src.at[strip - 1], dst_ref=dst.at[0], send_sem=send.at[1], recv_sem=recv.at[0],
            device_id=(my_t, my_r + 1), device_id_type=MESH)

    def halo_got(src, dst, send, recv, up):
        slot = 0 if up else 1
        return pltpu.make_async_remote_copy(
            src_ref=src.at[0], dst_ref=dst.at[slot], send_sem=send.at[slot], recv_sem=recv.at[slot],
            device_id=(my_t, my_r - 1 if up else my_r + 1), device_id_type=MESH)

    def send_halo(src, dst, send, recv):
        @pl.when(has_up)
        def _():
            halo(src, dst, send, recv, True).start()

        @pl.when(has_down)
        def _():
            halo(src, dst, send, recv, False).start()

    def halo_sent(src, dst, send, recv):
        @pl.when(has_up)
        def _():
            halo(src, dst, send, recv, True).wait_send()

        @pl.when(has_down)
        def _():
            halo(src, dst, send, recv, False).wait_send()

    def activate(src, edges, send, recv, scale, shift):
        def one(value):
            return silu(value.astype(F32) * scale + shift).astype(BF16)

        def body(w, carry):
            for r in range(strip):
                act[r + 1, w + 1] = one(src[r, w])
            return carry

        lax.fori_loop(0, W, body, 0, unroll=4)
        for up in (True, False):
            there = has_up if up else has_down
            slot, line = (0, 0) if up else (1, strip + 1)

            @pl.when(there)
            def _():
                halo_got(src, edges, send, recv, up).wait_recv()

                def edge(w, carry):
                    act[line, w + 1] = one(edges[slot, w])
                    return carry

                lax.fori_loop(0, W, edge, 0, unroll=4)

            @pl.when(jnp.logical_not(there))
            def _():
                act[line, 1 : W + 1] = jnp.zeros((W, F, C), BF16)

    def conv(r, weight):
        total = None
        for dy in range(3):
            for dx in range(3):
                window = act[r + dy, dx : dx + W].reshape(W * F, C)
                term = dot(window, weight[3 * dy + dx])
                total = term if total is None else total + term
        return total

    total, square = lax.fori_loop(0, W // 2, unpack, (zero, zero))
    put_stats(0, total, square)
    for r in range(strip + 2):
        act[r, 0] = jnp.zeros((F, C), BF16)
        act[r, W + 1] = jnp.zeros((F, C), BF16)
    pl.semaphore_wait(barrier, n - 1)
    send_stats(0)
    send_halo(xs, xh, hx_s, hx_r)

    def piece_copy(p):
        return pltpu.make_async_remote_copy(
            src_ref=panel.at[pl.ds(pl.multiple_of(p * PIECE, PIECE), PIECE)], dst_ref=land1.at[me],
            send_sem=l1_s.at[p], recv_sem=l1_r.at[me],
            device_id=(p // nr, lax.rem(p, nr)), device_id_type=MESH)

    def piece_start(off, carry):
        p = lax.rem(me + off, n)

        @pl.when(p < holders)
        def _():
            piece_copy(p).start()
        return carry

    lax.fori_loop(1, n, piece_start, 0)

    @pl.when(me < holders)
    def _():
        land1[me] = panel[pl.ds(pl.multiple_of(me * PIECE, PIECE), PIECE)]

    scale, shift = get_stats(0, row(0), row(1))
    activate(xs, xh, hx_s, hx_r, scale, shift)

    def conv_one(r, carry):
        total, square = carry
        value = (conv(r, k1) + row(2)).astype(BF16)
        hs[r] = value.reshape(W, F, C)
        wide = value.astype(F32).reshape(W, F, C)
        return total + jnp.sum(wide, axis=0), square + jnp.sum(wide * wide, axis=0)

    total, square = lax.fori_loop(0, strip, conv_one, (zero, zero))
    send_halo(hs, hh, hh_s, hh_r)
    put_stats(1, total, square)
    send_stats(1)

    def share_copy(dst):
        return pltpu.make_async_remote_copy(
            src_ref=src2.at[(dst // nr) // 2], dst_ref=land2.at[me],
            send_sem=l2_s.at[dst], recv_sem=l2_r.at[me],
            device_id=(dst // nr, lax.rem(dst, nr)), device_id_type=MESH)

    @pl.when(me < holders)
    def _():
        def piece_wait(off, carry):
            s = lax.rem(me + off, n)
            pltpu.make_async_remote_copy(
                src_ref=panel.at[pl.ds(0, PIECE)], dst_ref=land1.at[s],
                send_sem=l1_s.at[0], recv_sem=l1_r.at[s],
                device_id=(s // nr, lax.rem(s, nr)), device_id_type=MESH).wait_recv()
            return carry

        lax.fori_loop(1, n, piece_wait, 0)
        for k in range(clips):
            src2[k] = land1[choice[k]]
        land2[me] = src2[my_clip]

        def share(off, carry):
            share_copy(lax.rem(me + off, n)).start()
            return carry

        lax.fori_loop(1, n, share, 0)

    scale, shift = get_stats(1, row(3), row(4))
    activate(hs, hh, hh_s, hh_r, scale, shift)

    def conv_two(r, carry):
        total, square = carry
        value = conv(r, k2) + xs[r].reshape(W * F, C).astype(F32) + row(5)
        value = value.astype(BF16)
        res[r] = value.reshape(W, F, C)
        wide = value.astype(F32).reshape(W, F, C)
        return total + jnp.sum(wide, axis=0), square + jnp.sum(wide * wide, axis=0)

    total, square = lax.fori_loop(0, strip, conv_two, (zero, zero))
    put_stats(2, total, square)
    send_stats(2)

    def share_wait(off, carry):
        s = lax.rem(me + off, n)

        @pl.when(s < holders)
        def _():
            pltpu.make_async_remote_copy(
                src_ref=src2.at[0], dst_ref=land2.at[s],
                send_sem=l2_s.at[0], recv_sem=l2_r.at[s],
                device_id=(s // nr, lax.rem(s, nr)), device_id_type=MESH).wait_recv()
        return carry

    lax.fori_loop(1, n, share_wait, 0)
    degree = degrees[my_clip]
    kept = lax.broadcasted_iota(jnp.int32, (RANK, C), 0) < degree
    per = RANK // PIECE
    for j in range(4):
        down = land2[j * per : (j + 1) * per].reshape(RANK, C)
        down = jnp.where(kept, down.astype(F32), 0.0).astype(BF16)
        up = land2[(4 + j) * per : (5 + j) * per].reshape(RANK, C)
        pair = (up, down) if j == 2 else (down, up)
        weff[j] = (wa[j].astype(F32) + dot(pair[0], pair[1], ((0,), (0,)))).astype(BF16)

    scale, shift = get_stats(2, row(6), row(7))
    stamp = pe[pl.ds(pl.multiple_of(side * F, F), F)] + row(10)
    chunks = strip * W // CHUNK
    per_row = W // CHUNK

    def chunk_copy(c):
        return pltpu.make_async_remote_copy(
            src_ref=nown.at[c], dst_ref=npart.at[c], send_sem=n_s.at[c], recv_sem=n_r.at[c],
            device_id=(partner, my_r), device_id_type=MESH)

    def project(c, carry):
        r, w0 = c // per_row, lax.rem(c, per_row) * CHUNK
        u = (res[r, pl.ds(w0, CHUNK)].astype(F32) * scale + shift).astype(BF16)
        p = (dot(u.reshape(CHUNK * F, C), wi[...]) + row(8)).astype(BF16)
        proj[c] = p
        p = p.astype(F32)
        centre = p - jnp.sum(p, axis=-1, keepdims=True) * (1.0 / C)
        var = jnp.sum(centre * centre, axis=-1, keepdims=True) * (1.0 / C)
        layer = centre * lax.rsqrt(var + EPS) * row(9)
        layer = layer.reshape(CHUNK, F, C) + stamp
        nown[c] = layer.astype(BF16).reshape(CHUNK * F, C)
        chunk_copy(c).start()
        return carry

    lax.fori_loop(0, chunks, project, 0)

    rows = SUB * F
    key_pixel = lax.rem(lax.broadcasted_iota(jnp.int32, (2 * rows, rows), 0), rows) // F
    query_pixel = lax.broadcasted_iota(jnp.int32, (2 * rows, rows), 1) // F
    same = key_pixel == query_pixel
    lane = lax.broadcasted_iota(jnp.int32, (1, C), 1)
    root = 1.0 / math.sqrt(HD)

    def attend(c, carry):
        r, w0 = c // per_row, lax.rem(c, per_row) * CHUNK
        chunk_copy(c).wait_recv()
        for s in range(CHUNK // SUB):
            mine = nown[c, s * rows : (s + 1) * rows]
            theirs = npart[c, s * rows : (s + 1) * rows]
            both = jnp.concatenate([mine, theirs], axis=0)
            query = dot(mine, weff[0]).astype(BF16)
            keys = dot(both, weff[1]).astype(BF16)
            vals = dot(weff[2], both, ((1,), (1,))).astype(BF16).astype(F32)
            for h in range(HEADS):
                head = ((lane >= h * HD) & (lane < (h + 1) * HD)).astype(BF16)
                scores = dot(keys * head, query, ((1,), (1,)))
                scores = jnp.where(same, scores * root, -1e30)
                top = jnp.max(scores, axis=0, keepdims=True)
                power = jnp.exp(scores - top)
                total = jnp.sum(power, axis=0, keepdims=True)
                weights = (power * (1.0 / total)).astype(BF16)
                ot[h * HD : (h + 1) * HD, s * rows : (s + 1) * rows] = dot(
                    vals[h * HD : (h + 1) * HD].astype(BF16), weights)
        y = dot(ot[...].astype(BF16), weff[3], ((0,), (0,)))
        y = (y + proj[c].astype(F32) + row(11)).astype(BF16)
        final = dot(y, wo[...]) + res[r, pl.ds(w0, CHUNK)].reshape(CHUNK * F, C).astype(F32) + row(12)
        final = final.astype(BF16).reshape(CHUNK, F, C)
        for p in range(CHUNK // 2):
            two = jnp.concatenate([final[2 * p], final[2 * p + 1]], axis=-1)
            out[r, :, pl.ds(pl.multiple_of((w0 + 2 * p) * C, 128), 2 * C)] = two
        return carry

    lax.fori_loop(0, chunks, attend, 0)

    def sent(c, carry):
        chunk_copy(c).wait_send()
        return carry

    lax.fori_loop(0, chunks, sent, 0)
    for i in range(3):
        def step(off, carry):
            stat_copy(i, off).wait_send()
            return carry
        lax.fori_loop(1, nr, step, 0)
    halo_sent(xs, xh, hx_s, hx_r)
    halo_sent(hs, hh, hh_s, hh_r)

    def piece_sent(off, carry):
        p = lax.rem(me + off, n)

        @pl.when(p < holders)
        def _():
            piece_copy(p).wait_send()
        return carry

    lax.fori_loop(1, n, piece_sent, 0)

    @pl.when(me < holders)
    def _():
        def share_sent(off, carry):
            share_copy(lax.rem(me + off, n)).wait_send()
            return carry

        lax.fori_loop(1, n, share_sent, 0)


def per_device(
    latents, choice, degrees,
    gain1, shift1, k1, bias1, gain2, shift2, k2, bias2, gain3, shift3,
    wi, bi, ln_gain, ln_shift, wa, ab, lower, raise_, wo, ob,
):
    nt, nr = lax.axis_size("tm"), lax.axis_size("rows")
    n = nt * nr
    strip = latents.shape[1]
    clips = choice.shape[0]
    xt = jnp.transpose(latents, (1, 0, 2))
    vec = jnp.stack([gain1, shift1, bias1, gain2, shift2, bias2, gain3, shift3, bi, ln_gain, ln_shift, ab, ob])
    panel = jnp.concatenate(
        [jnp.transpose(lower[0], (0, 2, 1)).reshape(-1, C), raise_[0].reshape(-1, C)], axis=0)
    wa = jnp.stack([wa[0], wa[1], wa[2].T, wa[3]])
    vmem = pl.BlockSpec(memory_space=pltpu.VMEM)
    smem = pl.BlockSpec(memory_space=pltpu.SMEM)
    chunks = strip * W // CHUNK
    holders = min(PANEL_ROWS // PIECE, n)
    dma = pltpu.SemaphoreType.DMA
    out = pl.pallas_call(
        functools.partial(kernel, nt, nr, strip, clips),
        out_shape=jax.ShapeDtypeStruct(xt.shape, BF16),
        in_specs=[smem, smem] + [vmem] * 9,
        out_specs=vmem,
        scratch_shapes=[
            pltpu.VMEM((strip, W, F, C), BF16),
            pltpu.VMEM((2, W, F, C), BF16),
            pltpu.VMEM((strip, W, F, C), BF16),
            pltpu.VMEM((2, W, F, C), BF16),
            pltpu.VMEM((strip + 2, W + 2, F, C), BF16),
            pltpu.VMEM((strip, W, F, C), BF16),
            pltpu.VMEM((chunks, CHUNK * F, C), BF16),
            pltpu.VMEM((chunks, CHUNK * F, C), BF16),
            pltpu.VMEM((chunks, CHUNK * F, C), BF16),
            pltpu.VMEM((3, F, 128), F32),
            pltpu.VMEM((3, nr, F, 128), F32),
            pltpu.VMEM((n, PIECE, C), BF16),
            pltpu.VMEM((clips, PIECE, C), BF16),
            pltpu.VMEM((holders, PIECE, C), BF16),
            pltpu.VMEM((4, C, C), BF16),
            pltpu.VMEM((C, CHUNK * F), F32),
            pltpu.VMEM((8, 128), F32),
            dma((2,)), dma((2,)), dma((2,)), dma((2,)),
            dma((3, nr)), dma((3, nr)),
            dma((holders,)), dma((n,)), dma((n,)), dma((holders,)),
            dma((chunks,)), dma((chunks,)),
        ],
        compiler_params=pltpu.CompilerParams(
            collective_id=0, has_side_effects=True, vmem_limit_bytes=48 * 1024 * 1024),
        cost_estimate=pl.CostEstimate(flops=6 * 10**9, bytes_accessed=8 * 10**6, transcendentals=3 * 10**6),
    )(choice, degrees, xt, vec, jnp.asarray(positions()), k1.reshape(9, C, C), k2.reshape(9, C, C), wi, wa, wo, panel)
    return jnp.transpose(out, (1, 0, 2))


def solution(mesh):
    everywhere = P()
    in_specs = (
        (P("tm", "rows", None),) + (everywhere,) * 18
        + (P(("tm", "rows"), None, None, None),) * 2 + (everywhere,) * 2
    )
    return jax.shard_map(
        per_device, mesh=mesh, in_specs=in_specs, out_specs=P("tm", "rows", None), check_vma=False
    )
```

```python
import functools
import math

import jax
import jax.numpy as jnp
import numpy as np
from jax import lax
from jax.experimental import pallas as pl
from jax.experimental.pallas import tpu as pltpu
from jax.sharding import PartitionSpec as P

C = 320
GROUPS = 32
GS = 10
HEADS = 8
RANK = 64
W = 32
CLIP_LEN = 32
HD = 40
EPS = 1e-05
F = 16
PIECE = 16
PANEL_ROWS = 8 * RANK
CHUNK = 16
SUB = 8
MESH = pl.DeviceIdType.MESH
F32 = jnp.float32
BF16 = jnp.bfloat16
EXACT = lax.Precision.HIGHEST


def positions():
    index = np.arange(C)
    freq = np.exp(-(index // 2 * 2) * (math.log(10000.0) / C))
    angle = np.arange(CLIP_LEN)[:, None] * freq[None, :]
    return np.where(index[None, :] % 2 == 0, np.sin(angle), np.cos(angle)).astype(np.float32)


def dot(a, b, dims=((1,), (0,)), precision=None):
    return lax.dot_general(a, b, (dims, ((), ())), preferred_element_type=F32, precision=precision)


def silu(v):
    return 0.5 * v * (1.0 + jnp.tanh(0.5 * v))


def kernel(
    nt, nr, strip, clips,
    choice, degrees,
    xt, *refs,
):
    vec, refs = refs[:13], refs[13:]
    pe, k1, k2, wi, wa, wo, lower, upper, out, *refs = refs
    xs, xh, hs, hh, act, res, proj, nown, npart, ssrc, sland, land1, src2, land2, weff, ot, *refs = refs
    hx_s, hx_r, hh_s, hh_r, st_s, st_r, l1_s, l1_r, l2_s, l2_r, n_s, n_r = refs
    n = nt * nr
    pieces = PANEL_ROWS // PIECE
    holders = min(pieces, n)
    my_t = lax.axis_index("tm")
    my_r = lax.axis_index("rows")
    me = my_t * nr + my_r
    side = lax.rem(my_t, 2)
    partner = my_t + 1 - 2 * side
    my_clip = my_t // 2
    count = float(strip * nr * W * GS)
    has_up = my_r > 0
    has_down = my_r < nr - 1

    barrier = pltpu.get_barrier_semaphore()

    def greet(off, carry):
        dst = lax.rem(me + off, n)
        pl.semaphore_signal(barrier, inc=1, device_id=(dst // nr, lax.rem(dst, nr)), device_id_type=MESH)
        return carry

    lax.fori_loop(1, n, greet, 0)

    row = lambda i: vec[i][...].reshape(1, C)
    gc = lax.broadcasted_iota(jnp.int32, (C, 128), 0)
    gg = lax.broadcasted_iota(jnp.int32, (C, 128), 1) * GS
    to_first = ((gc >= gg) & (gc < gg + GS)).astype(F32)
    gg2 = gg - GROUPS * GS
    to_second = ((gc >= gg2) & (gc < gg2 + GS)).astype(F32)

    def unpack(p, carry):
        total, square = carry
        for r in range(strip):
            two = xt[r, :, pl.ds(pl.multiple_of(p * 2 * C, 128), 2 * C)]
            for i in range(2):
                one = two[:, i * C : (i + 1) * C]
                xs[r, 2 * p + i] = one
                wide = one.astype(F32)
                total = total + wide
                square = square + wide * wide
        return total, square

    zero = jnp.zeros((F, C), F32)

    def stat_copy(i, off):
        dst = lax.rem(my_r + off, nr)
        return pltpu.make_async_remote_copy(
            src_ref=ssrc.at[i], dst_ref=sland.at[i, my_r],
            send_sem=st_s.at[i, off], recv_sem=st_r.at[i, my_r],
            device_id=(my_t, dst), device_id_type=MESH)

    def stat_wait(i, off):
        src = lax.rem(my_r + off, nr)
        return pltpu.make_async_remote_copy(
            src_ref=ssrc.at[i], dst_ref=sland.at[i, src],
            send_sem=st_s.at[i, off], recv_sem=st_r.at[i, src],
            device_id=(my_t, src), device_id_type=MESH)

    def put_stats(i, total, square):
        mine = dot(total, to_first, precision=EXACT) + dot(square, to_second, precision=EXACT)
        ssrc[i] = mine
        sland[i, my_r] = mine

    def send_stats(i):
        def step(off, carry):
            stat_copy(i, off).start()
            return carry
        lax.fori_loop(1, nr, step, 0)

    def get_stats(i, gain, shift):
        def step(off, carry):
            stat_wait(i, off).wait_recv()
            return carry
        lax.fori_loop(1, nr, step, 0)
        total = sland[i, 0]
        for s in range(1, nr):
            total = total + sland[i, s]
        total = total * (1.0 / count)
        mean = dot(total, to_first, ((1,), (1,)), EXACT)
        var = dot(total, to_second, ((1,), (1,)), EXACT) - mean * mean
        scale = lax.rsqrt(var + EPS) * gain
        return scale, shift - mean * scale

    def halo(src, dst, send, recv, up):
        if up:
            return pltpu.make_async_remote_copy(
                src_ref=src.at[0], dst_ref=dst.at[1], send_sem=send.at[0], recv_sem=recv.at[1],
                device_id=(my_t, my_r - 1), device_id_type=MESH)
        return pltpu.make_async_remote_copy(
            src_ref=src.at[strip - 1], dst_ref=dst.at[0], send_sem=send.at[1], recv_sem=recv.at[0],
            device_id=(my_t, my_r + 1), device_id_type=MESH)

    def halo_got(src, dst, send, recv, up):
        slot = 0 if up else 1
        return pltpu.make_async_remote_copy(
            src_ref=src.at[0], dst_ref=dst.at[slot], send_sem=send.at[slot], recv_sem=recv.at[slot],
            device_id=(my_t, my_r - 1 if up else my_r + 1), device_id_type=MESH)

    def send_halo(src, dst, send, recv):
        @pl.when(has_up)
        def _():
            halo(src, dst, send, recv, True).start()

        @pl.when(has_down)
        def _():
            halo(src, dst, send, recv, False).start()

    def halo_sent(src, dst, send, recv):
        @pl.when(has_up)
        def _():
            halo(src, dst, send, recv, True).wait_send()

        @pl.when(has_down)
        def _():
            halo(src, dst, send, recv, False).wait_send()

    def activate(src, edges, send, recv, scale, shift):
        def one(value):
            return silu(value.astype(F32) * scale + shift).astype(BF16)

        def body(w, carry):
            for r in range(strip):
                act[r + 1, w + 1] = one(src[r, w])
            return carry

        lax.fori_loop(0, W, body, 0, unroll=4)
        for up in (True, False):
            there = has_up if up else has_down
            slot, line = (0, 0) if up else (1, strip + 1)

            @pl.when(there)
            def _():
                halo_got(src, edges, send, recv, up).wait_recv()

                def edge(w, carry):
                    act[line, w + 1] = one(edges[slot, w])
                    return carry

                lax.fori_loop(0, W, edge, 0, unroll=4)

            @pl.when(jnp.logical_not(there))
            def _():
                act[line, 1 : W + 1] = jnp.zeros((W, F, C), BF16)

    def conv(r, weight):
        total = None
        for dy in range(3):
            for dx in range(3):
                window = act[r + dy, dx : dx + W].reshape(W * F, C)
                term = dot(window, weight[3 * dy + dx])
                total = term if total is None else total + term
        return total

    total, square = lax.fori_loop(0, W // 2, unpack, (zero, zero))
    put_stats(0, total, square)
    for r in range(strip + 2):
        act[r, 0] = jnp.zeros((F, C), BF16)
        act[r, W + 1] = jnp.zeros((F, C), BF16)
    pl.semaphore_wait(barrier, n - 1)
    send_stats(0)
    send_halo(xs, xh, hx_s, hx_r)

    half = pieces // 2

    def rows_of(p):
        return pl.ds(pl.multiple_of(p * PIECE, PIECE), PIECE)

    def piece_copy(p, panel, first):
        return pltpu.make_async_remote_copy(
            src_ref=panel.at[rows_of(p - first)], dst_ref=land1.at[me],
            send_sem=l1_s.at[p], recv_sem=l1_r.at[me],
            device_id=(p // nr, lax.rem(p, nr)), device_id_type=MESH)

    def piece_start(off, carry):
        p = lax.rem(me + off, n)

        @pl.when(p < half)
        def _():
            piece_copy(p, lower, 0).start()

        @pl.when((p >= half) & (p < holders))
        def _():
            piece_copy(p, upper, half).start()
        return carry

    lax.fori_loop(1, n, piece_start, 0)

    @pl.when(me < half)
    def _():
        land1[me] = lower[rows_of(me)]

    @pl.when((me >= half) & (me < holders))
    def _():
        land1[me] = upper[rows_of(me - half)]

    scale, shift = get_stats(0, row(0), row(1))
    activate(xs, xh, hx_s, hx_r, scale, shift)

    def conv_one(r, carry):
        total, square = carry
        value = (conv(r, k1) + row(2)).astype(BF16)
        hs[r] = value.reshape(W, F, C)
        wide = value.astype(F32).reshape(W, F, C)
        return total + jnp.sum(wide, axis=0), square + jnp.sum(wide * wide, axis=0)

    total, square = lax.fori_loop(0, strip, conv_one, (zero, zero))
    send_halo(hs, hh, hh_s, hh_r)
    put_stats(1, total, square)
    send_stats(1)

    def share_copy(dst):
        return pltpu.make_async_remote_copy(
            src_ref=src2.at[(dst // nr) // 2], dst_ref=land2.at[me],
            send_sem=l2_s.at[dst], recv_sem=l2_r.at[me],
            device_id=(dst // nr, lax.rem(dst, nr)), device_id_type=MESH)

    @pl.when(me < holders)
    def _():
        def piece_wait(off, carry):
            s = lax.rem(me + off, n)
            pltpu.make_async_remote_copy(
                src_ref=lower.at[pl.ds(0, PIECE)], dst_ref=land1.at[s],
                send_sem=l1_s.at[0], recv_sem=l1_r.at[s],
                device_id=(s // nr, lax.rem(s, nr)), device_id_type=MESH).wait_recv()
            return carry

        lax.fori_loop(1, n, piece_wait, 0)
        for k in range(clips):
            src2[k] = land1[choice[k]]
        land2[me] = src2[my_clip]

        def share(off, carry):
            share_copy(lax.rem(me + off, n)).start()
            return carry

        lax.fori_loop(1, n, share, 0)

    scale, shift = get_stats(1, row(3), row(4))
    activate(hs, hh, hh_s, hh_r, scale, shift)

    def conv_two(r, carry):
        total, square = carry
        value = conv(r, k2) + xs[r].reshape(W * F, C).astype(F32) + row(5)
        value = value.astype(BF16)
        res[r] = value.reshape(W, F, C)
        wide = value.astype(F32).reshape(W, F, C)
        return total + jnp.sum(wide, axis=0), square + jnp.sum(wide * wide, axis=0)

    total, square = lax.fori_loop(0, strip, conv_two, (zero, zero))
    put_stats(2, total, square)
    send_stats(2)

    def share_wait(off, carry):
        s = lax.rem(me + off, n)

        @pl.when(s < holders)
        def _():
            pltpu.make_async_remote_copy(
                src_ref=src2.at[0], dst_ref=land2.at[s],
                send_sem=l2_s.at[0], recv_sem=l2_r.at[s],
                device_id=(s // nr, lax.rem(s, nr)), device_id_type=MESH).wait_recv()
        return carry

    lax.fori_loop(1, n, share_wait, 0)
    degree = degrees[my_clip]
    kept = lax.broadcasted_iota(jnp.int32, (RANK, C), 0) < degree
    per = RANK // PIECE
    for j in range(4):
        down = land2[j * per : (j + 1) * per].reshape(RANK, C)
        down = jnp.where(kept, down.astype(F32), 0.0).astype(BF16)
        up = land2[(4 + j) * per : (5 + j) * per].reshape(RANK, C)
        value = wa[j].astype(F32) + dot(down, up, ((0,), (0,)))
        weff[j] = (value.T if j == 2 else value).astype(BF16)

    scale, shift = get_stats(2, row(6), row(7))
    stamp = pe[pl.ds(pl.multiple_of(side * F, F), F)] + row(10)
    chunks = strip * W // CHUNK
    per_row = W // CHUNK

    def chunk_copy(c):
        return pltpu.make_async_remote_copy(
            src_ref=nown.at[c], dst_ref=npart.at[c], send_sem=n_s.at[c], recv_sem=n_r.at[c],
            device_id=(partner, my_r), device_id_type=MESH)

    def project(c, carry):
        r, w0 = c // per_row, lax.rem(c, per_row) * CHUNK
        u = (res[r, pl.ds(w0, CHUNK)].astype(F32) * scale + shift).astype(BF16)
        p = (dot(u.reshape(CHUNK * F, C), wi[...]) + row(8)).astype(BF16)
        proj[c] = p
        p = p.astype(F32)
        centre = p - jnp.sum(p, axis=-1, keepdims=True) * (1.0 / C)
        var = jnp.sum(centre * centre, axis=-1, keepdims=True) * (1.0 / C)
        layer = centre * lax.rsqrt(var + EPS) * row(9)
        layer = layer.reshape(CHUNK, F, C) + stamp
        nown[c] = layer.astype(BF16).reshape(CHUNK * F, C)
        chunk_copy(c).start()
        return carry

    lax.fori_loop(0, chunks, project, 0)

    rows = SUB * F
    key_pixel = lax.rem(lax.broadcasted_iota(jnp.int32, (2 * rows, rows), 0), rows) // F
    query_pixel = lax.broadcasted_iota(jnp.int32, (2 * rows, rows), 1) // F
    same = key_pixel == query_pixel
    lane = lax.broadcasted_iota(jnp.int32, (1, C), 1)
    root = 1.0 / math.sqrt(HD)

    def attend(c, carry):
        r, w0 = c // per_row, lax.rem(c, per_row) * CHUNK
        chunk_copy(c).wait_recv()
        for s in range(CHUNK // SUB):
            mine = nown[c, s * rows : (s + 1) * rows]
            theirs = npart[c, s * rows : (s + 1) * rows]
            both = jnp.concatenate([mine, theirs], axis=0)
            query = dot(mine, weff[0]).astype(BF16)
            keys = dot(both, weff[1]).astype(BF16)
            vals = dot(weff[2], both, ((1,), (1,))).astype(BF16).astype(F32)
            for h in range(HEADS):
                head = ((lane >= h * HD) & (lane < (h + 1) * HD)).astype(BF16)
                scores = dot(keys * head, query, ((1,), (1,)))
                scores = jnp.where(same, scores * root, -1e30)
                top = jnp.max(scores, axis=0, keepdims=True)
                power = jnp.exp(scores - top)
                total = jnp.sum(power, axis=0, keepdims=True)
                weights = (power * (1.0 / total)).astype(BF16)
                ot[h * HD : (h + 1) * HD, s * rows : (s + 1) * rows] = dot(
                    vals[h * HD : (h + 1) * HD].astype(BF16), weights)
        y = dot(ot[...].astype(BF16), weff[3], ((0,), (0,)))
        y = (y + proj[c].astype(F32) + row(11)).astype(BF16)
        final = dot(y, wo[...]) + res[r, pl.ds(w0, CHUNK)].reshape(CHUNK * F, C).astype(F32) + row(12)
        final = final.astype(BF16).reshape(CHUNK, F, C)
        for p in range(CHUNK // 2):
            two = jnp.concatenate([final[2 * p], final[2 * p + 1]], axis=-1)
            out[r, :, pl.ds(pl.multiple_of((w0 + 2 * p) * C, 128), 2 * C)] = two
        return carry

    lax.fori_loop(0, chunks, attend, 0)

    def sent(c, carry):
        chunk_copy(c).wait_send()
        return carry

    lax.fori_loop(0, chunks, sent, 0)
    for i in range(3):
        def step(off, carry):
            stat_copy(i, off).wait_send()
            return carry
        lax.fori_loop(1, nr, step, 0)
    halo_sent(xs, xh, hx_s, hx_r)
    halo_sent(hs, hh, hh_s, hh_r)

    def piece_sent(off, carry):
        p = lax.rem(me + off, n)

        @pl.when(p < holders)
        def _():
            piece_copy(p, lower, p).wait_send()
        return carry

    lax.fori_loop(1, n, piece_sent, 0)

    @pl.when(me < holders)
    def _():
        def share_sent(off, carry):
            share_copy(lax.rem(me + off, n)).wait_send()
            return carry

        lax.fori_loop(1, n, share_sent, 0)


def per_device(
    latents, choice, degrees,
    gain1, shift1, k1, bias1, gain2, shift2, k2, bias2, gain3, shift3,
    wi, bi, ln_gain, ln_shift, wa, ab, lower, raise_, wo, ob,
):
    nt, nr = lax.axis_size("tm"), lax.axis_size("rows")
    n = nt * nr
    strip = latents.shape[1]
    clips = choice.shape[0]
    xt = jnp.transpose(latents, (1, 0, 2))
    vec = [gain1, shift1, bias1, gain2, shift2, bias2, gain3, shift3, bi, ln_gain, ln_shift, ab, ob]
    lower = jnp.transpose(lower[0], (0, 2, 1)).reshape(-1, C)
    upper = raise_[0].reshape(-1, C)
    vmem = pl.BlockSpec(memory_space=pltpu.VMEM)
    smem = pl.BlockSpec(memory_space=pltpu.SMEM)
    chunks = strip * W // CHUNK
    holders = min(PANEL_ROWS // PIECE, n)
    dma = pltpu.SemaphoreType.DMA
    out = pl.pallas_call(
        functools.partial(kernel, nt, nr, strip, clips),
        out_shape=jax.ShapeDtypeStruct(xt.shape, BF16),
        in_specs=[smem, smem] + [vmem] * 22,
        out_specs=vmem,
        scratch_shapes=[
            pltpu.VMEM((strip, W, F, C), BF16),
            pltpu.VMEM((2, W, F, C), BF16),
            pltpu.VMEM((strip, W, F, C), BF16),
            pltpu.VMEM((2, W, F, C), BF16),
            pltpu.VMEM((strip + 2, W + 2, F, C), BF16),
            pltpu.VMEM((strip, W, F, C), BF16),
            pltpu.VMEM((chunks, CHUNK * F, C), BF16),
            pltpu.VMEM((chunks, CHUNK * F, C), BF16),
            pltpu.VMEM((chunks, CHUNK * F, C), BF16),
            pltpu.VMEM((3, F, 128), F32),
            pltpu.VMEM((3, nr, F, 128), F32),
            pltpu.VMEM((n, PIECE, C), BF16),
            pltpu.VMEM((clips, PIECE, C), BF16),
            pltpu.VMEM((holders, PIECE, C), BF16),
            pltpu.VMEM((4, C, C), BF16),
            pltpu.VMEM((C, CHUNK * F), F32),
            dma((2,)), dma((2,)), dma((2,)), dma((2,)),
            dma((3, nr)), dma((3, nr)),
            dma((holders,)), dma((n,)), dma((n,)), dma((holders,)),
            dma((chunks,)), dma((chunks,)),
        ],
        compiler_params=pltpu.CompilerParams(
            collective_id=0, has_side_effects=True, vmem_limit_bytes=48 * 1024 * 1024),
        cost_estimate=pl.CostEstimate(flops=6 * 10**9, bytes_accessed=8 * 10**6, transcendentals=3 * 10**6),
    )(
        choice, degrees, xt, *vec, jnp.asarray(positions()),
        k1.reshape(9, C, C), k2.reshape(9, C, C), wi, wa, wo, lower, upper)
    return jnp.transpose(out, (1, 0, 2))


def solution(mesh):
    everywhere = P()
    in_specs = (
        (P("tm", "rows", None),) + (everywhere,) * 18
        + (P(("tm", "rows"), None, None, None),) * 2 + (everywhere,) * 2
    )
    return jax.shard_map(
        per_device, mesh=mesh, in_specs=in_specs, out_specs=P("tm", "rows", None), check_vma=False
    )
```

```python
import functools
import math

import jax
import jax.numpy as jnp
import numpy as np
from jax import lax
from jax.experimental import pallas as pl
from jax.experimental.pallas import tpu as pltpu
from jax.sharding import PartitionSpec as P

C = 320
GROUPS = 32
GS = 10
HEADS = 8
RANK = 64
W = 32
CLIP_LEN = 32
HD = 40
EPS = 1e-05
F = 16
PANEL_ROWS = 8 * RANK
CHUNK = 16
SUB = 8
MESH = pl.DeviceIdType.MESH
F32 = jnp.float32
BF16 = jnp.bfloat16
EXACT = lax.Precision.HIGHEST


def positions():
    index = np.arange(C)
    freq = np.exp(-(index // 2 * 2) * (math.log(10000.0) / C))
    angle = np.arange(CLIP_LEN)[:, None] * freq[None, :]
    return np.where(index[None, :] % 2 == 0, np.sin(angle), np.cos(angle)).astype(np.float32)


def dot(a, b, dims=((1,), (0,)), precision=None):
    return lax.dot_general(a, b, (dims, ((), ())), preferred_element_type=F32, precision=precision)


def silu(v):
    return 0.5 * v * (1.0 + jnp.tanh(0.5 * v))


def kernel(
    nt, nr, strip, clips,
    choice, degrees,
    xt, *refs,
):
    far, refs = refs[:19], refs[19:]
    lower, upper, out, *refs = refs
    near, refs = refs[:19], refs[19:]
    vec = near[:13]
    pe, k1, k2, wi, wa, wo = near[13:]
    load_sem, own_sem, *refs = refs
    xs, xh, hs, hh, act, res, proj, nown, npart, ssrc, sland, land1, src2, mid, src3, land2, weff, ot, *refs = refs
    hx_s, hx_r, hh_s, hh_r, st_s, st_r, l1_s, l1_r, lm_s, lm_r, l2_s, l2_r, n_s, n_r = refs
    piece = PANEL_ROWS // nr
    my_t = lax.axis_index("tm")
    my_r = lax.axis_index("rows")
    side = lax.rem(my_t, 2)
    partner = my_t + 1 - 2 * side
    my_clip = my_t // 2
    count = float(strip * nr * W * GS)
    has_up = my_r > 0
    has_down = my_r < nr - 1

    barrier = pltpu.get_barrier_semaphore()

    def greet_row(off, carry):
        pl.semaphore_signal(barrier, inc=1, device_id=(my_t, lax.rem(my_r + off, nr)), device_id_type=MESH)
        return carry

    def greet_column(off, carry):
        pl.semaphore_signal(barrier, inc=1, device_id=(lax.rem(my_t + off, nt), my_r), device_id_type=MESH)
        return carry

    lax.fori_loop(1, nr, greet_row, 0)
    lax.fori_loop(1, nt, greet_column, 0)

    loads = [pltpu.make_async_copy(a, b, load_sem.at[i]) for i, (a, b) in enumerate(zip(far, near))]
    for i in (*range(13), 14, 15, 13, 16, 17, 18):
        loads[i].start()

    row = lambda i: vec[i][...].reshape(1, C)
    gc = lax.broadcasted_iota(jnp.int32, (C, 128), 0)
    gg = lax.broadcasted_iota(jnp.int32, (C, 128), 1) * GS
    to_first = ((gc >= gg) & (gc < gg + GS)).astype(F32)
    gg2 = gg - GROUPS * GS
    to_second = ((gc >= gg2) & (gc < gg2 + GS)).astype(F32)

    def unpack(p, carry):
        total, square = carry
        for r in range(strip):
            two = xt[r, :, pl.ds(pl.multiple_of(p * 2 * C, 128), 2 * C)]
            for i in range(2):
                one = two[:, i * C : (i + 1) * C]
                xs[r, 2 * p + i] = one
                wide = one.astype(F32)
                total = total + wide
                square = square + wide * wide
        return total, square

    zero = jnp.zeros((F, C), F32)

    def stat_copy(i, off):
        dst = lax.rem(my_r + off, nr)
        return pltpu.make_async_remote_copy(
            src_ref=ssrc.at[i], dst_ref=sland.at[i, my_r],
            send_sem=st_s.at[i, off], recv_sem=st_r.at[i, my_r],
            device_id=(my_t, dst), device_id_type=MESH)

    def stat_wait(i, off):
        src = lax.rem(my_r + off, nr)
        return pltpu.make_async_remote_copy(
            src_ref=ssrc.at[i], dst_ref=sland.at[i, src],
            send_sem=st_s.at[i, off], recv_sem=st_r.at[i, src],
            device_id=(my_t, src), device_id_type=MESH)

    def put_stats(i, total, square):
        mine = dot(total, to_first, precision=EXACT) + dot(square, to_second, precision=EXACT)
        ssrc[i] = mine
        sland[i, my_r] = mine

    def send_stats(i):
        def step(off, carry):
            stat_copy(i, off).start()
            return carry
        lax.fori_loop(1, nr, step, 0)

    def get_stats(i, gain, shift):
        def step(off, carry):
            stat_wait(i, off).wait_recv()
            return carry
        lax.fori_loop(1, nr, step, 0)
        total = sland[i, 0]
        for s in range(1, nr):
            total = total + sland[i, s]
        total = total * (1.0 / count)
        mean = dot(total, to_first, ((1,), (1,)), EXACT)
        var = dot(total, to_second, ((1,), (1,)), EXACT) - mean * mean
        scale = lax.rsqrt(var + EPS) * gain
        return scale, shift - mean * scale

    def halo(src, dst, send, recv, up):
        if up:
            return pltpu.make_async_remote_copy(
                src_ref=src.at[0], dst_ref=dst.at[1], send_sem=send.at[0], recv_sem=recv.at[1],
                device_id=(my_t, my_r - 1), device_id_type=MESH)
        return pltpu.make_async_remote_copy(
            src_ref=src.at[strip - 1], dst_ref=dst.at[0], send_sem=send.at[1], recv_sem=recv.at[0],
            device_id=(my_t, my_r + 1), device_id_type=MESH)

    def halo_got(src, dst, send, recv, up):
        slot = 0 if up else 1
        return pltpu.make_async_remote_copy(
            src_ref=src.at[0], dst_ref=dst.at[slot], send_sem=send.at[slot], recv_sem=recv.at[slot],
            device_id=(my_t, my_r - 1 if up else my_r + 1), device_id_type=MESH)

    def send_halo(src, dst, send, recv):
        @pl.when(has_up)
        def _():
            halo(src, dst, send, recv, True).start()

        @pl.when(has_down)
        def _():
            halo(src, dst, send, recv, False).start()

    def halo_sent(src, dst, send, recv):
        @pl.when(has_up)
        def _():
            halo(src, dst, send, recv, True).wait_send()

        @pl.when(has_down)
        def _():
            halo(src, dst, send, recv, False).wait_send()

    def activate(src, edges, send, recv, scale, shift):
        def one(value):
            return silu(value.astype(F32) * scale + shift).astype(BF16)

        def body(w, carry):
            for r in range(strip):
                act[r + 1, w + 1] = one(src[r, w])
            return carry

        lax.fori_loop(0, W, body, 0, unroll=4)
        for up in (True, False):
            there = has_up if up else has_down
            slot, line = (0, 0) if up else (1, strip + 1)

            @pl.when(there)
            def _():
                halo_got(src, edges, send, recv, up).wait_recv()

                def edge(w, carry):
                    act[line, w + 1] = one(edges[slot, w])
                    return carry

                lax.fori_loop(0, W, edge, 0, unroll=4)

            @pl.when(jnp.logical_not(there))
            def _():
                act[line, 1 : W + 1] = jnp.zeros((W, F, C), BF16)

    def conv(r, weight):
        total = None
        for dy in range(3):
            for dx in range(3):
                window = act[r + dy, dx : dx + W].reshape(W * F, C)
                term = dot(window, weight[3 * dy + dx])
                total = term if total is None else total + term
        return total

    total, square = lax.fori_loop(0, W // 2, unpack, (zero, zero))
    put_stats(0, total, square)
    for r in range(strip + 2):
        act[r, 0] = jnp.zeros((F, C), BF16)
        act[r, W + 1] = jnp.zeros((F, C), BF16)
    pl.semaphore_wait(barrier, nr + nt - 2)
    send_stats(0)
    send_halo(xs, xh, hx_s, hx_r)

    half = nr // 2

    def rows_of(p):
        return pl.ds(pl.multiple_of(p * piece, piece), piece)

    def piece_copy(p, panel, first):
        return pltpu.make_async_remote_copy(
            src_ref=panel.at[rows_of(p - first)], dst_ref=land1.at[my_r],
            send_sem=l1_s.at[p], recv_sem=l1_r.at[my_r],
            device_id=(my_t, p), device_id_type=MESH)

    def piece_start(off, carry):
        p = lax.rem(my_r + off, nr)

        @pl.when(p < half)
        def _():
            piece_copy(p, lower, 0).start()

        @pl.when(p >= half)
        def _():
            piece_copy(p, upper, half).start()
        return carry

    lax.fori_loop(1, nr, piece_start, 0)

    def own_piece(panel, first):
        return pltpu.make_async_copy(panel.at[rows_of(my_r - first)], land1.at[my_r], own_sem.at[0])

    @pl.when(my_r < half)
    def _():
        own_piece(lower, 0).start()

    @pl.when(my_r >= half)
    def _():
        own_piece(upper, half).start()

    for i in range(13):
        loads[i].wait()
    scale, shift = get_stats(0, row(0), row(1))
    activate(xs, xh, hx_s, hx_r, scale, shift)

    loads[14].wait()

    def conv_one(r, carry):
        total, square = carry
        value = (conv(r, k1) + row(2)).astype(BF16)
        hs[r] = value.reshape(W, F, C)
        wide = value.astype(F32).reshape(W, F, C)
        return total + jnp.sum(wide, axis=0), square + jnp.sum(wide * wide, axis=0)

    total, square = lax.fori_loop(0, strip, conv_one, (zero, zero))
    send_halo(hs, hh, hh_s, hh_r)
    put_stats(1, total, square)
    send_stats(1)

    def pass_copy(t):
        return pltpu.make_async_remote_copy(
            src_ref=src2.at[t // 2], dst_ref=mid.at[my_t], send_sem=lm_s.at[t], recv_sem=lm_r.at[my_t],
            device_id=(t, my_r), device_id_type=MESH)

    def piece_wait(off, carry):
        p = lax.rem(my_r + off, nr)
        pltpu.make_async_remote_copy(
            src_ref=lower.at[pl.ds(0, piece)], dst_ref=land1.at[p],
            send_sem=l1_s.at[p], recv_sem=l1_r.at[p],
            device_id=(my_t, p), device_id_type=MESH).wait_recv()
        return carry

    lax.fori_loop(1, nr, piece_wait, 0)
    own_piece(lower, my_r).wait()
    for k in range(clips):
        src2[k] = land1[lax.rem(choice[k], nr)]
    mid[my_t] = src2[my_clip]

    def pass_start(off, carry):
        pass_copy(lax.rem(my_t + off, nt)).start()
        return carry

    lax.fori_loop(1, nt, pass_start, 0)

    scale, shift = get_stats(1, row(3), row(4))
    activate(hs, hh, hh_s, hh_r, scale, shift)

    def share_copy(p):
        return pltpu.make_async_remote_copy(
            src_ref=src3, dst_ref=land2.at[my_r], send_sem=l2_s.at[p], recv_sem=l2_r.at[my_r],
            device_id=(my_t, p), device_id_type=MESH)

    def pass_wait(off, carry):
        t = lax.rem(my_t + off, nt)
        pltpu.make_async_remote_copy(
            src_ref=src2.at[0], dst_ref=mid.at[t], send_sem=lm_s.at[t], recv_sem=lm_r.at[t],
            device_id=(t, my_r), device_id_type=MESH).wait_recv()
        return carry

    lax.fori_loop(1, nt, pass_wait, 0)
    chosen = mid[choice[my_clip] // nr]
    src3[...] = chosen
    land2[my_r] = chosen

    def share_start(off, carry):
        share_copy(lax.rem(my_r + off, nr)).start()
        return carry

    lax.fori_loop(1, nr, share_start, 0)
    loads[15].wait()

    def conv_two(r, carry):
        total, square = carry
        value = conv(r, k2) + xs[r].reshape(W * F, C).astype(F32) + row(5)
        value = value.astype(BF16)
        res[r] = value.reshape(W, F, C)
        wide = value.astype(F32).reshape(W, F, C)
        return total + jnp.sum(wide, axis=0), square + jnp.sum(wide * wide, axis=0)

    total, square = lax.fori_loop(0, strip, conv_two, (zero, zero))
    put_stats(2, total, square)
    send_stats(2)

    def share_wait(off, carry):
        p = lax.rem(my_r + off, nr)
        pltpu.make_async_remote_copy(
            src_ref=src3, dst_ref=land2.at[p], send_sem=l2_s.at[p], recv_sem=l2_r.at[p],
            device_id=(my_t, p), device_id_type=MESH).wait_recv()
        return carry

    lax.fori_loop(1, nr, share_wait, 0)
    for i in (13, 16, 17, 18):
        loads[i].wait()
    degree = degrees[my_clip]
    kept = lax.broadcasted_iota(jnp.int32, (RANK, C), 0) < degree
    per = RANK // piece
    for j in range(4):
        down = land2[j * per : (j + 1) * per].reshape(RANK, C)
        down = jnp.where(kept, down.astype(F32), 0.0).astype(BF16)
        up = land2[(4 + j) * per : (5 + j) * per].reshape(RANK, C)
        value = wa[j].astype(F32) + dot(down, up, ((0,), (0,)))
        weff[j] = (value.T if j == 2 else value).astype(BF16)

    scale, shift = get_stats(2, row(6), row(7))
    stamp = pe[pl.ds(pl.multiple_of(side * F, F), F)] + row(10)
    chunks = strip * W // CHUNK
    per_row = W // CHUNK

    def chunk_copy(c):
        return pltpu.make_async_remote_copy(
            src_ref=nown.at[c], dst_ref=npart.at[c], send_sem=n_s.at[c], recv_sem=n_r.at[c],
            device_id=(partner, my_r), device_id_type=MESH)

    def project(c, carry):
        r, w0 = c // per_row, lax.rem(c, per_row) * CHUNK
        u = (res[r, pl.ds(w0, CHUNK)].astype(F32) * scale + shift).astype(BF16)
        p = (dot(u.reshape(CHUNK * F, C), wi[...]) + row(8)).astype(BF16)
        proj[c] = p
        p = p.astype(F32)
        centre = p - jnp.sum(p, axis=-1, keepdims=True) * (1.0 / C)
        var = jnp.sum(centre * centre, axis=-1, keepdims=True) * (1.0 / C)
        layer = centre * lax.rsqrt(var + EPS) * row(9)
        layer = layer.reshape(CHUNK, F, C) + stamp
        nown[c] = layer.astype(BF16).reshape(CHUNK * F, C)
        chunk_copy(c).start()
        return carry

    lax.fori_loop(0, chunks, project, 0)

    rows = SUB * F
    key_pixel = lax.rem(lax.broadcasted_iota(jnp.int32, (2 * rows, rows), 0), rows) // F
    query_pixel = lax.broadcasted_iota(jnp.int32, (2 * rows, rows), 1) // F
    same = key_pixel == query_pixel
    lane = lax.broadcasted_iota(jnp.int32, (1, C), 1)
    root = 1.0 / math.sqrt(HD)

    def attend(c, carry):
        r, w0 = c // per_row, lax.rem(c, per_row) * CHUNK
        chunk_copy(c).wait_recv()
        for s in range(CHUNK // SUB):
            mine = nown[c, s * rows : (s + 1) * rows]
            theirs = npart[c, s * rows : (s + 1) * rows]
            both = jnp.concatenate([mine, theirs], axis=0)
            query = dot(mine, weff[0]).astype(BF16)
            keys = dot(both, weff[1]).astype(BF16)
            vals = dot(weff[2], both, ((1,), (1,))).astype(BF16).astype(F32)
            for h in range(HEADS):
                head = ((lane >= h * HD) & (lane < (h + 1) * HD)).astype(BF16)
                scores = dot(keys * head, query, ((1,), (1,)))
                scores = jnp.where(same, scores * root, -1e30)
                top = jnp.max(scores, axis=0, keepdims=True)
                power = jnp.exp(scores - top)
                total = jnp.sum(power, axis=0, keepdims=True)
                weights = (power * (1.0 / total)).astype(BF16)
                ot[h * HD : (h + 1) * HD, s * rows : (s + 1) * rows] = dot(
                    vals[h * HD : (h + 1) * HD].astype(BF16), weights)
        y = dot(ot[...].astype(BF16), weff[3], ((0,), (0,)))
        y = (y + proj[c].astype(F32) + row(11)).astype(BF16)
        final = dot(y, wo[...]) + res[r, pl.ds(w0, CHUNK)].reshape(CHUNK * F, C).astype(F32) + row(12)
        final = final.astype(BF16).reshape(CHUNK, F, C)
        for p in range(CHUNK // 2):
            two = jnp.concatenate([final[2 * p], final[2 * p + 1]], axis=-1)
            out[r, :, pl.ds(pl.multiple_of((w0 + 2 * p) * C, 128), 2 * C)] = two
        return carry

    lax.fori_loop(0, chunks, attend, 0)

    def sent(c, carry):
        chunk_copy(c).wait_send()
        return carry

    lax.fori_loop(0, chunks, sent, 0)
    for i in range(3):
        def step(off, carry):
            stat_copy(i, off).wait_send()
            return carry
        lax.fori_loop(1, nr, step, 0)
    halo_sent(xs, xh, hx_s, hx_r)
    halo_sent(hs, hh, hh_s, hh_r)

    def piece_sent(off, carry):
        p = lax.rem(my_r + off, nr)
        piece_copy(p, lower, p).wait_send()
        share_copy(p).wait_send()
        return carry

    def pass_sent(off, carry):
        pass_copy(lax.rem(my_t + off, nt)).wait_send()
        return carry

    lax.fori_loop(1, nr, piece_sent, 0)
    lax.fori_loop(1, nt, pass_sent, 0)


def per_device(
    latents, choice, degrees,
    gain1, shift1, k1, bias1, gain2, shift2, k2, bias2, gain3, shift3,
    wi, bi, ln_gain, ln_shift, wa, ab, lower, raise_, wo, ob,
):
    nt, nr = lax.axis_size("tm"), lax.axis_size("rows")
    strip = latents.shape[1]
    clips = choice.shape[0]
    xt = jnp.transpose(latents, (1, 0, 2))
    vec = [gain1, shift1, bias1, gain2, shift2, bias2, gain3, shift3, bi, ln_gain, ln_shift, ab, ob]
    lower = jnp.transpose(lower[0], (0, 2, 1)).reshape(-1, C)
    upper = raise_[0].reshape(-1, C)
    vmem = pl.BlockSpec(memory_space=pltpu.VMEM)
    smem = pl.BlockSpec(memory_space=pltpu.SMEM)
    chunks = strip * W // CHUNK
    piece = PANEL_ROWS // nr
    dma = pltpu.SemaphoreType.DMA
    params = [*vec, jnp.asarray(positions()), k1.reshape(9, C, C), k2.reshape(9, C, C), wi, wa, wo]
    out = pl.pallas_call(
        functools.partial(kernel, nt, nr, strip, clips),
        out_shape=jax.ShapeDtypeStruct(xt.shape, BF16),
        in_specs=[smem, smem, vmem] + [pl.BlockSpec(memory_space=pltpu.HBM)] * 21,
        out_specs=vmem,
        scratch_shapes=[pltpu.VMEM(a.shape, a.dtype) for a in params] + [
            dma((len(params),)), dma((1,)),
            pltpu.VMEM((strip, W, F, C), BF16),
            pltpu.VMEM((2, W, F, C), BF16),
            pltpu.VMEM((strip, W, F, C), BF16),
            pltpu.VMEM((2, W, F, C), BF16),
            pltpu.VMEM((strip + 2, W + 2, F, C), BF16),
            pltpu.VMEM((strip, W, F, C), BF16),
            pltpu.VMEM((chunks, CHUNK * F, C), BF16),
            pltpu.VMEM((chunks, CHUNK * F, C), BF16),
            pltpu.VMEM((chunks, CHUNK * F, C), BF16),
            pltpu.VMEM((3, F, 128), F32),
            pltpu.VMEM((3, nr, F, 128), F32),
            pltpu.VMEM((nr, piece, C), BF16),
            pltpu.VMEM((clips, piece, C), BF16),
            pltpu.VMEM((nt, piece, C), BF16),
            pltpu.VMEM((piece, C), BF16),
            pltpu.VMEM((nr, piece, C), BF16),
            pltpu.VMEM((4, C, C), BF16),
            pltpu.VMEM((C, CHUNK * F), F32),
            dma((2,)), dma((2,)), dma((2,)), dma((2,)),
            dma((3, nr)), dma((3, nr)),
            dma((nr,)), dma((nr,)), dma((nt,)), dma((nt,)), dma((nr,)), dma((nr,)),
            dma((chunks,)), dma((chunks,)),
        ],
        compiler_params=pltpu.CompilerParams(
            collective_id=0, has_side_effects=True, vmem_limit_bytes=64 * 1024 * 1024),
        cost_estimate=pl.CostEstimate(flops=6 * 10**9, bytes_accessed=8 * 10**6, transcendentals=3 * 10**6),
    )(
        choice, degrees, xt, *params, lower, upper)
    return jnp.transpose(out, (1, 0, 2))


def solution(mesh):
    everywhere = P()
    in_specs = (
        (P("tm", "rows", None),) + (everywhere,) * 18
        + (P(("tm", "rows"), None, None, None),) * 2 + (everywhere,) * 2
    )
    return jax.shard_map(
        per_device, mesh=mesh, in_specs=in_specs, out_specs=P("tm", "rows", None), check_vma=False
    )
```

```python
import functools
import math

import jax
import jax.numpy as jnp
import numpy as np
from jax import lax
from jax.experimental import pallas as pl
from jax.experimental.pallas import tpu as pltpu
from jax.sharding import PartitionSpec as P

C = 320
GROUPS = 32
GS = 10
HEADS = 8
RANK = 64
W = 32
CLIP_LEN = 32
HD = 40
EPS = 1e-05
F = 16
PANEL_ROWS = 8 * RANK
CHUNK = 16
SUB = 8
MESH = pl.DeviceIdType.MESH
F32 = jnp.float32
BF16 = jnp.bfloat16
EXACT = lax.Precision.HIGHEST


def positions():
    index = np.arange(C)
    freq = np.exp(-(index // 2 * 2) * (math.log(10000.0) / C))
    angle = np.arange(CLIP_LEN)[:, None] * freq[None, :]
    return np.where(index[None, :] % 2 == 0, np.sin(angle), np.cos(angle)).astype(np.float32)


def dot(a, b, dims=((1,), (0,)), precision=None):
    return lax.dot_general(a, b, (dims, ((), ())), preferred_element_type=F32, precision=precision)


def silu(v):
    return 0.5 * v * (1.0 + jnp.tanh(0.5 * v))


def kernel(
    nt, nr, strip, clips,
    choice, degrees,
    xt, *refs,
):
    far, refs = refs[:19], refs[19:]
    lower, upper, out, *refs = refs
    near, refs = refs[:19], refs[19:]
    vec = near[:13]
    pe, k1, k2, wi, wa, wo = near[13:]
    load_sem, own_sem, *refs = refs
    xs, xh, hs, hh, act, res, proj, nown, npart, ssrc, sland, land1, src2, mid, src3, land2, weff, ot, *refs = refs
    hx_s, hx_r, hh_s, hh_r, st_s, st_r, l1_s, l1_r, lm_s, lm_r, l2_s, l2_r, n_s, n_r = refs
    piece = PANEL_ROWS // nr
    my_t = lax.axis_index("tm")
    my_r = lax.axis_index("rows")
    side = lax.rem(my_t, 2)
    partner = my_t + 1 - 2 * side
    my_clip = my_t // 2
    count = float(strip * nr * W * GS)
    has_up = my_r > 0
    has_down = my_r < nr - 1

    barrier = pltpu.get_barrier_semaphore()

    def greet_row(off, carry):
        pl.semaphore_signal(barrier, inc=1, device_id=(my_t, lax.rem(my_r + off, nr)), device_id_type=MESH)
        return carry

    def greet_column(off, carry):
        pl.semaphore_signal(barrier, inc=1, device_id=(lax.rem(my_t + off, nt), my_r), device_id_type=MESH)
        return carry

    lax.fori_loop(1, nr, greet_row, 0)
    lax.fori_loop(1, nt, greet_column, 0)

    loads = [pltpu.make_async_copy(a, b, load_sem.at[i]) for i, (a, b) in enumerate(zip(far, near))]
    for i in (*range(13), 14, 15, 13, 16, 17, 18):
        loads[i].start()

    row = lambda i: vec[i][...].reshape(1, C)
    gc = lax.broadcasted_iota(jnp.int32, (C, 128), 0)
    gg = lax.broadcasted_iota(jnp.int32, (C, 128), 1) * GS
    to_first = ((gc >= gg) & (gc < gg + GS)).astype(F32)
    gg2 = gg - GROUPS * GS
    to_second = ((gc >= gg2) & (gc < gg2 + GS)).astype(F32)

    def unpack(p, carry):
        total, square = carry
        for r in range(strip):
            two = xt[r, :, pl.ds(pl.multiple_of(p * 2 * C, 128), 2 * C)]
            for i in range(2):
                one = two[:, i * C : (i + 1) * C]
                xs[r, 2 * p + i] = one
                wide = one.astype(F32)
                total = total + wide
                square = square + wide * wide
        return total, square

    zero = jnp.zeros((F, C), F32)

    def stat_copy(i, off):
        dst = lax.rem(my_r + off, nr)
        return pltpu.make_async_remote_copy(
            src_ref=ssrc.at[i], dst_ref=sland.at[i, my_r],
            send_sem=st_s.at[i, off], recv_sem=st_r.at[i, my_r],
            device_id=(my_t, dst), device_id_type=MESH)

    def stat_wait(i, off):
        src = lax.rem(my_r + off, nr)
        return pltpu.make_async_remote_copy(
            src_ref=ssrc.at[i], dst_ref=sland.at[i, src],
            send_sem=st_s.at[i, off], recv_sem=st_r.at[i, src],
            device_id=(my_t, src), device_id_type=MESH)

    def put_stats(i, total, square):
        mine = dot(total, to_first, precision=EXACT) + dot(square, to_second, precision=EXACT)
        ssrc[i] = mine
        sland[i, my_r] = mine

    def send_stats(i):
        def step(off, carry):
            stat_copy(i, off).start()
            return carry
        lax.fori_loop(1, nr, step, 0, unroll=True)

    def get_stats(i, gain, shift):
        def step(off, carry):
            stat_wait(i, off).wait_recv()
            return carry
        lax.fori_loop(1, nr, step, 0, unroll=True)
        total = sland[i, 0]
        for s in range(1, nr):
            total = total + sland[i, s]
        total = total * (1.0 / count)
        mean = dot(total, to_first, ((1,), (1,)), EXACT)
        var = dot(total, to_second, ((1,), (1,)), EXACT) - mean * mean
        scale = lax.rsqrt(var + EPS) * gain
        return scale, shift - mean * scale

    def halo(src, dst, send, recv, up):
        if up:
            return pltpu.make_async_remote_copy(
                src_ref=src.at[0], dst_ref=dst.at[1], send_sem=send.at[0], recv_sem=recv.at[1],
                device_id=(my_t, my_r - 1), device_id_type=MESH)
        return pltpu.make_async_remote_copy(
            src_ref=src.at[strip - 1], dst_ref=dst.at[0], send_sem=send.at[1], recv_sem=recv.at[0],
            device_id=(my_t, my_r + 1), device_id_type=MESH)

    def halo_got(src, dst, send, recv, up):
        slot = 0 if up else 1
        return pltpu.make_async_remote_copy(
            src_ref=src.at[0], dst_ref=dst.at[slot], send_sem=send.at[slot], recv_sem=recv.at[slot],
            device_id=(my_t, my_r - 1 if up else my_r + 1), device_id_type=MESH)

    def send_halo(src, dst, send, recv):
        @pl.when(has_up)
        def _():
            halo(src, dst, send, recv, True).start()

        @pl.when(has_down)
        def _():
            halo(src, dst, send, recv, False).start()

    def halo_sent(src, dst, send, recv):
        @pl.when(has_up)
        def _():
            halo(src, dst, send, recv, True).wait_send()

        @pl.when(has_down)
        def _():
            halo(src, dst, send, recv, False).wait_send()

    def activate(src, edges, send, recv, scale, shift):
        def one(value):
            return silu(value.astype(F32) * scale + shift).astype(BF16)

        def body(w, carry):
            for r in range(strip):
                act[r + 1, w + 1] = one(src[r, w])
            return carry

        lax.fori_loop(0, W, body, 0, unroll=4)
        for up in (True, False):
            there = has_up if up else has_down
            slot, line = (0, 0) if up else (1, strip + 1)

            @pl.when(there)
            def _():
                halo_got(src, edges, send, recv, up).wait_recv()

                def edge(w, carry):
                    act[line, w + 1] = one(edges[slot, w])
                    return carry

                lax.fori_loop(0, W, edge, 0, unroll=4)

            @pl.when(jnp.logical_not(there))
            def _():
                act[line, 1 : W + 1] = jnp.zeros((W, F, C), BF16)

    def conv(r, weight):
        total = None
        for dy in range(3):
            for dx in range(3):
                window = act[r + dy, dx : dx + W].reshape(W * F, C)
                term = dot(window, weight[3 * dy + dx])
                total = term if total is None else total + term
        return total

    total, square = lax.fori_loop(0, W // 2, unpack, (zero, zero), unroll=2)
    put_stats(0, total, square)
    for r in range(strip + 2):
        act[r, 0] = jnp.zeros((F, C), BF16)
        act[r, W + 1] = jnp.zeros((F, C), BF16)
    pl.semaphore_wait(barrier, nr + nt - 2)
    send_stats(0)
    send_halo(xs, xh, hx_s, hx_r)

    half = nr // 2

    def rows_of(p):
        return pl.ds(pl.multiple_of(p * piece, piece), piece)

    def piece_copy(p, panel, first):
        return pltpu.make_async_remote_copy(
            src_ref=panel.at[rows_of(p - first)], dst_ref=land1.at[my_r],
            send_sem=l1_s.at[p], recv_sem=l1_r.at[my_r],
            device_id=(my_t, p), device_id_type=MESH)

    def piece_start(off, carry):
        p = lax.rem(my_r + off, nr)

        @pl.when(p < half)
        def _():
            piece_copy(p, lower, 0).start()

        @pl.when(p >= half)
        def _():
            piece_copy(p, upper, half).start()
        return carry

    lax.fori_loop(1, nr, piece_start, 0)

    def own_piece(panel, first):
        return pltpu.make_async_copy(panel.at[rows_of(my_r - first)], land1.at[my_r], own_sem.at[0])

    @pl.when(my_r < half)
    def _():
        own_piece(lower, 0).start()

    @pl.when(my_r >= half)
    def _():
        own_piece(upper, half).start()

    for i in range(13):
        loads[i].wait()
    scale, shift = get_stats(0, row(0), row(1))
    activate(xs, xh, hx_s, hx_r, scale, shift)

    loads[14].wait()

    def conv_one(r, carry):
        total, square = carry
        value = (conv(r, k1) + row(2)).astype(BF16)
        hs[r] = value.reshape(W, F, C)
        wide = value.astype(F32).reshape(W, F, C)
        return total + jnp.sum(wide, axis=0), square + jnp.sum(wide * wide, axis=0)

    total, square = lax.fori_loop(0, strip, conv_one, (zero, zero))
    send_halo(hs, hh, hh_s, hh_r)
    put_stats(1, total, square)
    send_stats(1)

    def pass_copy(t):
        return pltpu.make_async_remote_copy(
            src_ref=src2.at[t // 2], dst_ref=mid.at[my_t], send_sem=lm_s.at[t], recv_sem=lm_r.at[my_t],
            device_id=(t, my_r), device_id_type=MESH)

    def piece_wait(off, carry):
        p = lax.rem(my_r + off, nr)
        pltpu.make_async_remote_copy(
            src_ref=lower.at[pl.ds(0, piece)], dst_ref=land1.at[p],
            send_sem=l1_s.at[p], recv_sem=l1_r.at[p],
            device_id=(my_t, p), device_id_type=MESH).wait_recv()
        return carry

    lax.fori_loop(1, nr, piece_wait, 0)
    own_piece(lower, my_r).wait()
    for k in range(clips):
        src2[k] = land1[lax.rem(choice[k], nr)]
    mid[my_t] = src2[my_clip]

    def pass_start(off, carry):
        pass_copy(lax.rem(my_t + off, nt)).start()
        return carry

    lax.fori_loop(1, nt, pass_start, 0)

    scale, shift = get_stats(1, row(3), row(4))
    activate(hs, hh, hh_s, hh_r, scale, shift)

    def share_copy(p):
        return pltpu.make_async_remote_copy(
            src_ref=src3, dst_ref=land2.at[my_r], send_sem=l2_s.at[p], recv_sem=l2_r.at[my_r],
            device_id=(my_t, p), device_id_type=MESH)

    def pass_wait(off, carry):
        t = lax.rem(my_t + off, nt)
        pltpu.make_async_remote_copy(
            src_ref=src2.at[0], dst_ref=mid.at[t], send_sem=lm_s.at[t], recv_sem=lm_r.at[t],
            device_id=(t, my_r), device_id_type=MESH).wait_recv()
        return carry

    lax.fori_loop(1, nt, pass_wait, 0)
    chosen = mid[choice[my_clip] // nr]
    src3[...] = chosen
    land2[my_r] = chosen

    def share_start(off, carry):
        share_copy(lax.rem(my_r + off, nr)).start()
        return carry

    lax.fori_loop(1, nr, share_start, 0)
    loads[15].wait()

    def conv_two(r, carry):
        total, square = carry
        value = conv(r, k2) + xs[r].reshape(W * F, C).astype(F32) + row(5)
        value = value.astype(BF16)
        res[r] = value.reshape(W, F, C)
        wide = value.astype(F32).reshape(W, F, C)
        return total + jnp.sum(wide, axis=0), square + jnp.sum(wide * wide, axis=0)

    total, square = lax.fori_loop(0, strip, conv_two, (zero, zero))
    put_stats(2, total, square)
    send_stats(2)

    def share_wait(off, carry):
        p = lax.rem(my_r + off, nr)
        pltpu.make_async_remote_copy(
            src_ref=src3, dst_ref=land2.at[p], send_sem=l2_s.at[p], recv_sem=l2_r.at[p],
            device_id=(my_t, p), device_id_type=MESH).wait_recv()
        return carry

    lax.fori_loop(1, nr, share_wait, 0)
    for i in (13, 16, 17, 18):
        loads[i].wait()
    degree = degrees[my_clip]
    kept = lax.broadcasted_iota(jnp.int32, (RANK, C), 0) < degree
    per = RANK // piece
    for j in range(4):
        down = land2[j * per : (j + 1) * per].reshape(RANK, C)
        down = jnp.where(kept, down.astype(F32), 0.0).astype(BF16)
        up = land2[(4 + j) * per : (5 + j) * per].reshape(RANK, C)
        value = wa[j].astype(F32) + dot(down, up, ((0,), (0,)))
        weff[j] = (value.T if j == 2 else value).astype(BF16)

    scale, shift = get_stats(2, row(6), row(7))
    stamp = pe[pl.ds(pl.multiple_of(side * F, F), F)] + row(10)
    chunks = strip * W // CHUNK
    per_row = W // CHUNK

    def chunk_copy(c):
        return pltpu.make_async_remote_copy(
            src_ref=nown.at[c], dst_ref=npart.at[c], send_sem=n_s.at[c], recv_sem=n_r.at[c],
            device_id=(partner, my_r), device_id_type=MESH)

    def project(c, carry):
        r, w0 = c // per_row, lax.rem(c, per_row) * CHUNK
        u = (res[r, pl.ds(w0, CHUNK)].astype(F32) * scale + shift).astype(BF16)
        p = (dot(u.reshape(CHUNK * F, C), wi[...]) + row(8)).astype(BF16)
        proj[c] = p
        p = p.astype(F32)
        centre = p - jnp.sum(p, axis=-1, keepdims=True) * (1.0 / C)
        var = jnp.sum(centre * centre, axis=-1, keepdims=True) * (1.0 / C)
        layer = centre * lax.rsqrt(var + EPS) * row(9)
        layer = layer.reshape(CHUNK, F, C) + stamp
        nown[c] = layer.astype(BF16).reshape(CHUNK * F, C)
        chunk_copy(c).start()
        return carry

    lax.fori_loop(0, chunks, project, 0, unroll=2)

    rows = SUB * F
    key_pixel = lax.rem(lax.broadcasted_iota(jnp.int32, (2 * rows, rows), 0), rows) // F
    query_pixel = lax.broadcasted_iota(jnp.int32, (2 * rows, rows), 1) // F
    same = key_pixel == query_pixel
    lane = lax.broadcasted_iota(jnp.int32, (1, C), 1)
    root = 1.0 / math.sqrt(HD)

    def attend(c, carry):
        r, w0 = c // per_row, lax.rem(c, per_row) * CHUNK
        chunk_copy(c).wait_recv()
        for s in range(CHUNK // SUB):
            mine = nown[c, s * rows : (s + 1) * rows]
            theirs = npart[c, s * rows : (s + 1) * rows]
            both = jnp.concatenate([mine, theirs], axis=0)
            query = dot(mine, weff[0]).astype(BF16)
            keys = dot(both, weff[1]).astype(BF16)
            vals = dot(weff[2], both, ((1,), (1,))).astype(BF16).astype(F32)
            for h in range(HEADS):
                head = ((lane >= h * HD) & (lane < (h + 1) * HD)).astype(BF16)
                scores = dot(keys * head, query, ((1,), (1,)))
                scores = jnp.where(same, scores * root, -1e30)
                top = jnp.max(scores, axis=0, keepdims=True)
                power = jnp.exp(scores - top)
                total = jnp.sum(power, axis=0, keepdims=True)
                weights = (power * (1.0 / total)).astype(BF16)
                ot[h * HD : (h + 1) * HD, s * rows : (s + 1) * rows] = dot(
                    vals[h * HD : (h + 1) * HD].astype(BF16), weights)
        y = dot(ot[...].astype(BF16), weff[3], ((0,), (0,)))
        y = (y + proj[c].astype(F32) + row(11)).astype(BF16)
        final = dot(y, wo[...]) + res[r, pl.ds(w0, CHUNK)].reshape(CHUNK * F, C).astype(F32) + row(12)
        final = final.astype(BF16).reshape(CHUNK, F, C)
        for p in range(CHUNK // 2):
            two = jnp.concatenate([final[2 * p], final[2 * p + 1]], axis=-1)
            out[r, :, pl.ds(pl.multiple_of((w0 + 2 * p) * C, 128), 2 * C)] = two
        return carry

    lax.fori_loop(0, chunks, attend, 0)

    def sent(c, carry):
        chunk_copy(c).wait_send()
        return carry

    lax.fori_loop(0, chunks, sent, 0)
    for i in range(3):
        def step(off, carry):
            stat_copy(i, off).wait_send()
            return carry
        lax.fori_loop(1, nr, step, 0, unroll=True)
    halo_sent(xs, xh, hx_s, hx_r)
    halo_sent(hs, hh, hh_s, hh_r)

    def piece_sent(off, carry):
        p = lax.rem(my_r + off, nr)
        piece_copy(p, lower, p).wait_send()
        share_copy(p).wait_send()
        return carry

    def pass_sent(off, carry):
        pass_copy(lax.rem(my_t + off, nt)).wait_send()
        return carry

    lax.fori_loop(1, nr, piece_sent, 0)
    lax.fori_loop(1, nt, pass_sent, 0)


def per_device(
    latents, choice, degrees,
    gain1, shift1, k1, bias1, gain2, shift2, k2, bias2, gain3, shift3,
    wi, bi, ln_gain, ln_shift, wa, ab, lower, raise_, wo, ob,
):
    nt, nr = lax.axis_size("tm"), lax.axis_size("rows")
    strip = latents.shape[1]
    clips = choice.shape[0]
    xt = jnp.transpose(latents, (1, 0, 2))
    vec = [gain1, shift1, bias1, gain2, shift2, bias2, gain3, shift3, bi, ln_gain, ln_shift, ab, ob]
    lower = jnp.transpose(lower[0], (0, 2, 1)).reshape(-1, C)
    upper = raise_[0].reshape(-1, C)
    vmem = pl.BlockSpec(memory_space=pltpu.VMEM)
    smem = pl.BlockSpec(memory_space=pltpu.SMEM)
    chunks = strip * W // CHUNK
    piece = PANEL_ROWS // nr
    dma = pltpu.SemaphoreType.DMA
    params = [*vec, jnp.asarray(positions()), k1.reshape(9, C, C), k2.reshape(9, C, C), wi, wa, wo]
    out = pl.pallas_call(
        functools.partial(kernel, nt, nr, strip, clips),
        out_shape=jax.ShapeDtypeStruct(xt.shape, BF16),
        in_specs=[smem, smem, vmem] + [pl.BlockSpec(memory_space=pltpu.HBM)] * 21,
        out_specs=vmem,
        scratch_shapes=[pltpu.VMEM(a.shape, a.dtype) for a in params] + [
            dma((len(params),)), dma((1,)),
            pltpu.VMEM((strip, W, F, C), BF16),
            pltpu.VMEM((2, W, F, C), BF16),
            pltpu.VMEM((strip, W, F, C), BF16),
            pltpu.VMEM((2, W, F, C), BF16),
            pltpu.VMEM((strip + 2, W + 2, F, C), BF16),
            pltpu.VMEM((strip, W, F, C), BF16),
            pltpu.VMEM((chunks, CHUNK * F, C), BF16),
            pltpu.VMEM((chunks, CHUNK * F, C), BF16),
            pltpu.VMEM((chunks, CHUNK * F, C), BF16),
            pltpu.VMEM((3, F, 128), F32),
            pltpu.VMEM((3, nr, F, 128), F32),
            pltpu.VMEM((nr, piece, C), BF16),
            pltpu.VMEM((clips, piece, C), BF16),
            pltpu.VMEM((nt, piece, C), BF16),
            pltpu.VMEM((piece, C), BF16),
            pltpu.VMEM((nr, piece, C), BF16),
            pltpu.VMEM((4, C, C), BF16),
            pltpu.VMEM((C, CHUNK * F), F32),
            dma((2,)), dma((2,)), dma((2,)), dma((2,)),
            dma((3, nr)), dma((3, nr)),
            dma((nr,)), dma((nr,)), dma((nt,)), dma((nt,)), dma((nr,)), dma((nr,)),
            dma((chunks,)), dma((chunks,)),
        ],
        compiler_params=pltpu.CompilerParams(
            collective_id=0, has_side_effects=True, vmem_limit_bytes=64 * 1024 * 1024),
        cost_estimate=pl.CostEstimate(flops=6 * 10**9, bytes_accessed=8 * 10**6, transcendentals=3 * 10**6),
    )(
        choice, degrees, xt, *params, lower, upper)
    return jnp.transpose(out, (1, 0, 2))


def solution(mesh):
    everywhere = P()
    in_specs = (
        (P("tm", "rows", None),) + (everywhere,) * 18
        + (P(("tm", "rows"), None, None, None),) * 2 + (everywhere,) * 2
    )
    return jax.shard_map(
        per_device, mesh=mesh, in_specs=in_specs, out_specs=P("tm", "rows", None), check_vma=False
    )
```
